128 devices in a mesh: expert: 16 (over x, z), hidden: 8 (over y, core).
Axes of the slice: x: 4, y: 4, z: 4, core: 2. Of those that a mesh axis runs over, the one named last changes fastest.
Arguments:
- tokens: bfloat16 [8192, 3072], P('expert'), may hold values from -6 to 6
- out_grad: bfloat16 [8192, 3072], P('expert'), may hold values from -1.5 to 1.5
- gates: bfloat16 [8192, 8], P('expert'), may hold values from 0.19921875 to 1
- labels: int32 [8192], P('expert'), may hold values from 0 to 1, as said below
- text_picks: int32 [8, 512], replicated, may hold values from 0 to 4095, as said below
- image_picks: int32 [8, 256], replicated, may hold values from 0 to 4095, as said below
- block_mask: int32 [16, 64], P('expert', 'hidden'), may hold values 0 or 1
- w_gate: bfloat16 [16, 3072, 8192], P('expert', None, 'hidden'), may hold values from -0.109375 to 0.109375
- w_up: bfloat16 [16, 3072, 8192], P('expert', None, 'hidden'), may hold values from -0.109375 to 0.109375
- w_down: bfloat16 [16, 8192, 3072], P('expert', 'hidden'), may hold values from -0.0625 to 0.0625
Outputs:
- input_grad: bfloat16 [8192, 3072], P('expert', 'hidden')
- router_grad: bfloat16 [8192, 8], P('expert')
The draws below stay inside these ranges and needn't reach their ends.
Inputs may be any that keep to these rules, and one draw needn't show every extreme that they name: `labels`: exactly 256 of the 512 tokens on each index of expert are text (0); the others are image (1). `text_picks`: ranks count the text tokens in order of index of expert, then position. Each row names 512 different ranks, at most 48 of them among the text tokens of one index of expert, and exactly 48 for some index. `image_picks`: ranks count the image tokens in order of index of expert, then position. Each row names 256 different ranks, at most 24 of them among the image tokens of one index of expert, and exactly 24 for some index.
All inputs are finite; a program needn't handle non-finite values. No bound on the sum of `block_mask` on one device may be relied on, other than what follows from the above.
Results may differ from the reference program's by a relative error of at most 0.02.
Values may be sent and summed in bfloat16 or wider, within the bound.
A program may use at most 128 MiB of HBM per device.

```python
import jax
import jax.numpy as jnp
from jax import lax

D = 3072
FF = 8192
BLK = 128
TOK_DEV = 512
EXPERTS = 16
E_HALF = 8
HGROUPS = 8
TOKENS = 8192
HALF = 256
CAP_T = 512
CAP_I = 256
SLOT = 48


def pick_ranks(key, capacity):
    mean_count = capacity // EXPERTS
    spread_most = mean_count // 2

    def one_expert(expert_key):
        pair_key, size_key, local_key, shuffle_key = jax.random.split(expert_key, 4)
        sources = jax.random.permutation(pair_key, EXPERTS)
        spread = jax.random.randint(size_key, (EXPERTS // 2,), 0, spread_most + 1).astype(jnp.int32)
        spread = spread.at[0].set(spread_most)
        counts = jnp.zeros((EXPERTS,), jnp.int32).at[sources[0::2]].set(mean_count + spread)
        counts = counts.at[sources[1::2]].set(mean_count - spread)
        local_keys = jax.random.split(local_key, EXPERTS)
        local_ranks = jax.vmap(lambda sub_key: jax.random.permutation(sub_key, HALF)[:SLOT])(local_keys)
        in_count = jnp.arange(SLOT, dtype=jnp.int32)[None, :] < counts[:, None]
        all_ranks = jnp.arange(EXPERTS, dtype=jnp.int32)[:, None] * HALF + local_ranks.astype(jnp.int32)
        chosen = jnp.argsort(jnp.where(in_count, 0, 1).reshape(-1), stable=True)[:capacity]
        picked = all_ranks.reshape(-1)[chosen]
        return picked[jax.random.permutation(shuffle_key, capacity)].astype(jnp.int32)
    return jax.vmap(one_expert)(jax.random.split(key, E_HALF))


def draw_labels(key, part):
    key = jax.random.fold_in(key, 7)
    block_keys = jax.random.split(key, EXPERTS)
    blocks = jax.vmap(lambda block_key: (jax.random.permutation(block_key, TOK_DEV) >= HALF).astype(jnp.int32))(block_keys)
    return blocks.reshape(TOKENS)


def draw_text_picks(key, part):
    key = jax.random.fold_in(key, 11)
    return pick_ranks(key, CAP_T)


def draw_image_picks(key, part):
    key = jax.random.fold_in(key, 13)
    return pick_ranks(key, CAP_I)


def plant(entries, stream_key, smallest, largest):
    dims = entries.shape
    place = [jax.random.randint(jax.random.fold_in(stream_key, axis), (), 0, dims[axis]) for axis in range(len(dims))]
    entries = entries.at[tuple(place)].set(smallest)
    longest = dims.index(max(dims))
    place[longest] = (place[longest] + 1) % dims[longest]
    return entries.at[tuple(place)].set(largest)


def block_levels(stream_key, dims, pieces, smallest, top_value):
    loudness = 1.0
    for position, parts in pieces:
        steps = jax.random.uniform(jax.random.fold_in(jax.random.fold_in(stream_key, 6), position), (parts,), jnp.float32, smallest / len(pieces), top_value / len(pieces))
        loudness = loudness * jnp.repeat(jnp.exp(steps), dims[position] // parts).reshape((-1,) + (1,) * (len(dims) - 1 - position))
    return loudness


def scatter_about(own_key, dims, width, most, cuts=(), kind=jnp.bfloat16):
    factor_of = block_levels(own_key, dims, cuts, -0.22, 0.18) if cuts else 1.0
    entries = jax.random.normal(own_key, dims, jnp.float32) * width * factor_of
    return jnp.minimum(jnp.maximum(entries, -most), most).astype(kind)


def setup_inputs(seed: int = 0) -> dict:
    key_of = jax.random.split(jax.random.key(seed), 11)
    return {
        "tokens": scatter_about(key_of[0], (TOKENS, D), 1.0, 6.0, ((0, 16),)),
        "out_grad": scatter_about(key_of[1], (TOKENS, D), 0.25, 1.5, ((0, 16),)),
        "gates": jnp.clip(0.19921875 + 0.80078125 * jax.random.uniform(key_of[2], (TOKENS, E_HALF), jnp.float32) ** block_levels(key_of[2], (TOKENS, E_HALF), ((0, 16),), -0.2, 0.2), 0.19921875, 1.0).astype(jnp.bfloat16),
        "labels": draw_labels(jax.random.fold_in(key_of[10], 71), 0),
        "text_picks": draw_text_picks(jax.random.fold_in(key_of[10], 71), 0),
        "image_picks": draw_image_picks(jax.random.fold_in(key_of[10], 71), 0),
        "block_mask": plant((jax.random.randint(key_of[6], (EXPERTS, FF // BLK), 0, 4) < 3).astype(jnp.int32), jax.random.fold_in(key_of[6], 1), 0, 1),
        "w_gate": scatter_about(key_of[7], (EXPERTS, D, FF), D ** -0.5, 0.109375, ((0, 16), (2, 8))),
        "w_up": scatter_about(key_of[8], (EXPERTS, D, FF), D ** -0.5, 0.109375, ((0, 16), (2, 8))),
        "w_down": scatter_about(key_of[9], (EXPERTS, FF, D), FF ** -0.5, 0.0625, ((0, 16), (1, 8))),
    }


def swish_parts(pre_gate):
    sigmoid_gate = jax.nn.sigmoid(pre_gate)
    return pre_gate * sigmoid_gate, sigmoid_gate * (1.0 + pre_gate * (1.0 - sigmoid_gate))


def expert_grads(tokens, out_grad, gates, picked, column, weight_gate, weight_up, weight_down, mask_row):
    token_rows = tokens[picked]
    grad_rows = out_grad[picked]
    scale_rows = gates[picked, column].astype(jnp.float32)
    gate_in = jnp.dot(token_rows, weight_gate, preferred_element_type=jnp.float32)
    up_in = jnp.dot(token_rows, weight_up, preferred_element_type=jnp.float32)
    block_keep = jnp.repeat(mask_row.astype(jnp.float32), BLK)
    swish, swish_slope = swish_parts(gate_in)
    activation = (swish * up_in * block_keep).astype(jnp.bfloat16)
    back_proj = jnp.dot(grad_rows, weight_down.T, preferred_element_type=jnp.float32)
    score_grad = jnp.sum(activation.astype(jnp.float32) * back_proj, axis=1).astype(jnp.bfloat16)
    hidden_grad = scale_rows[:, None] * back_proj * block_keep
    gate_delta = (hidden_grad * up_in * swish_slope).astype(jnp.bfloat16)
    up_delta = (hidden_grad * swish).astype(jnp.bfloat16)
    row_total = picked.shape[0]
    group_width = FF // HGROUPS
    gate_groups = gate_delta.reshape(row_total, HGROUPS, group_width).astype(jnp.float32)
    up_groups = up_delta.reshape(row_total, HGROUPS, group_width).astype(jnp.float32)
    gate_weights = weight_gate.reshape(D, HGROUPS, group_width).astype(jnp.float32)
    up_weights = weight_up.reshape(D, HGROUPS, group_width).astype(jnp.float32)
    partial_value = jnp.einsum("chf,dhf->hcd", gate_groups, gate_weights) + jnp.einsum("chf,dhf->hcd", up_groups, up_weights)
    partial_value = partial_value.astype(jnp.bfloat16)
    row_grad = jnp.sum(partial_value.astype(jnp.float32), axis=0).astype(jnp.bfloat16)
    return row_grad, score_grad


def reference(tokens, out_grad, gates, labels, text_picks, image_picks, block_mask, w_gate, w_up, w_down):
    token_order = jnp.argsort(labels, stable=True).astype(jnp.int32)
    text_rows = token_order[text_picks]
    image_rows = token_order[TOKENS // 2 + image_picks]
    columns = jnp.arange(E_HALF, dtype=jnp.int32)

    def step_fn(totals, inputs):
        grad_sum, router = totals
        picked, column, weight_gate, weight_up, weight_down, mask_row = inputs
        row_grad, score_grad = expert_grads(tokens, out_grad, gates, picked, column, weight_gate, weight_up, weight_down, mask_row)
        grad_sum = grad_sum.at[picked].add(row_grad.astype(jnp.float32))
        router = router.at[picked, column].add(score_grad.astype(jnp.float32))
        return (grad_sum, router), None

    totals = (jnp.zeros((TOKENS, D), jnp.float32), jnp.zeros((TOKENS, E_HALF), jnp.float32))
    totals, _ = lax.scan(step_fn, totals, (text_rows, columns, w_gate[:E_HALF], w_up[:E_HALF], w_down[:E_HALF], block_mask[:E_HALF]))
    totals, _ = lax.scan(step_fn, totals, (image_rows, columns, w_gate[E_HALF:], w_up[E_HALF:], w_down[E_HALF:], block_mask[E_HALF:]))
    return totals[0].astype(jnp.bfloat16), totals[1].astype(jnp.bfloat16)
```

```python
import jax
import jax.numpy as jnp
from jax import lax
from jax.experimental import pallas as pl
from jax.experimental.pallas import tpu as pltpu
from jax.sharding import PartitionSpec as P

MESH = pl.DeviceIdType.MESH
F32 = jnp.float32
BF16 = jnp.bfloat16

TD = 512
HALF = 256
NE = 16
EH = 8
SL = 48
SI = 24
NS = NE * SL
D = 3072
FB = 384
YB = 768
FH = 1024
RC = 256


def nt(a, b):
    return lax.dot_general(a, b, (((1,), (1,)), ((), ())), preferred_element_type=F32)


def nn(a, b):
    return jnp.dot(a, b, preferred_element_type=F32)


def iota(shape, dim):
    return lax.broadcasted_iota(jnp.int32, shape, dim)


def one(cond):
    return jnp.where(cond, 1.0, 0.0).astype(F32)


def kernel(
    tok_h, og_h, gates, labels, tpk, ipk, mask, wg_h, wu_h, wd_h,
    ig, rg,
    wg, wu, wd, cols, tri, idn, mref, smat, s2mat, gmat, omat, pmat, ptmat,
    send_t, send_i, recv, x, acc, gd, ud, stage, crecv, fstage, ustage, dstage,
    arecv, brecv, urecv, drecv, rgm, vsend, vrecv, srecv, scs, scr,
    ld_sem, w_sem, s1t, s1i, r1, sy, ry, sc, rc, ss, rs, scc, rcc, sab, rab, sud, rud,
    sv, rv, sq, rq,
):
    me = lax.axis_index("expert")
    h = lax.axis_index("hidden")
    y = lax.div(h, 2)
    c = lax.rem(h, 2)
    oc = 1 - c
    far = lax.rem(y + 2, 4)
    up = lax.rem(y + 1, 4)
    dn = lax.rem(y + 3, 4)
    kcol = lax.rem(me, EH)
    is_text = me < EH
    n_chunks = 2 - lax.div(me, EH)
    blocks = (y, far, up, dn)

    def remote(src, dst, s_sem, r_sem, **where):
        return pltpu.make_async_remote_copy(
            src_ref=src, dst_ref=dst, send_sem=s_sem, recv_sem=r_sem,
            device_id=where, device_id_type=MESH,
        )

    def colsl(core):
        return pl.ds(pl.multiple_of(core * FB, 128), FB)

    def rowsl(r):
        return pl.ds(pl.multiple_of(r * RC, RC), RC)

    loads = []
    for f, yy in enumerate((y, far)):
        fs = pl.ds(pl.multiple_of((yy * 2 + c) * FB, 128), FB)
        for a, src in enumerate((tok_h, og_h)):
            cp = pltpu.make_async_copy(
                src.at[:, fs], cols.at[f, pl.ds(a * TD, TD), :], ld_sem.at[f, a])
            cp.start()
            loads.append(cp)
    wloads = []
    for k, yy in enumerate(blocks):
        rows = pl.ds(pl.multiple_of(yy * YB, YB), YB)
        trio = [
            pltpu.make_async_copy(wg_h.at[rows, :], wg.at[rows, :], w_sem.at[k, 0]),
            pltpu.make_async_copy(wu_h.at[rows, :], wu.at[rows, :], w_sem.at[k, 1]),
            pltpu.make_async_copy(wd_h.at[:, rows], wd.at[:, rows], w_sem.at[k, 2]),
        ]
        for cp in trio:
            cp.start()
        wloads.append(trio)

    barrier = pltpu.get_barrier_semaphore()

    @pl.loop(1, NE)
    def _(k):
        pl.semaphore_signal(barrier, inc=1, device_id={"expert": lax.rem(me + k, NE)}, device_id_type=MESH)

    @pl.loop(1, 8)
    def _(k):
        pl.semaphore_signal(barrier, inc=1, device_id={"hidden": lax.rem(h + k, 8)}, device_id_type=MESH)

    r5 = iota((TD, TD), 0)
    c5 = iota((TD, TD), 1)
    tri[...] = one(r5 <= c5).astype(BF16)
    idn[...] = one(r5 == c5).astype(BF16)
    text = one(labels[...] == 0)
    lab16 = jnp.where(iota((NE, TD), 0) < EH, text, 1.0 - text)
    rank = nn(lab16.astype(BF16), tri[...])
    key = jnp.where(lab16 > 0.0, rank - 1.0, -1.0)

    def local_rank(p):
        return jnp.where(lax.shift_right_logical(p, 8) == me, (p & 255), -1).astype(F32)

    lov = jnp.concatenate([
        local_rank(tpk[...]),
        jnp.concatenate([local_rank(ipk[...]), jnp.full((EH, TD - HALF), -1.0, F32)], axis=1),
    ], axis=0)
    lov_t = nt(idn[...], lov.astype(BF16))
    rrow = iota((1, HALF), 1).astype(F32)
    for e in range(NE):
        depth = TD if e < EH else HALF
        hit = one(lov_t[:depth, e:e + 1] == rrow)
        mref[e:e + 1, :] = jnp.sum(hit, axis=0, keepdims=True)
    member = mref[...]
    slot1 = member * nn(member.astype(BF16), tri[:HALF, :HALF])
    slot1 = slot1.astype(BF16)
    rcol = iota((HALF, TD), 0).astype(F32)
    st_text = nn(slot1, one(rcol == key[0:1, :]).astype(BF16))
    st_image = nn(slot1, one(rcol == key[EH:EH + 1, :]).astype(BF16))
    st = jnp.where(iota((NE, TD), 0) < EH, st_text, st_image)
    s1 = iota((SL, TD), 0).astype(F32) + 1.0
    for e in range(EH):
        smat[e * SL:(e + 1) * SL, :] = one(st[e:e + 1, :] == s1).astype(BF16)
        im = st[EH + e:EH + e + 1, :]
        s2mat[e * SL:(e + 1) * SL, :TD] = one(im == s1).astype(BF16)
        im2 = jnp.where(im > 0.0, im + SI, -1.0)
        s2mat[e * SL:(e + 1) * SL, TD:] = one(im2 == s1).astype(BF16)

    pl.semaphore_wait(barrier, NE - 1 + 7)

    def text_copy(f, a, d):
        return remote(send_t.at[f, a, d], recv.at[f, a, me], s1t.at[f, a, d], r1.at[f, a, me], expert=d)

    def image_copy(f, d):
        return remote(send_i.at[f, d], recv.at[f, 0, me], s1i.at[f, d], r1.at[f, 0, me], expert=EH + d)

    for f in range(2):
        for a in range(2):
            loads[f * 2 + a].wait()
            t = nn(smat[...], cols[f, a * TD:(a + 1) * TD, :])
            send_t[f, a] = t.astype(BF16).reshape(EH, SL, FB)

            @pl.loop(0, EH)
            def _(k):
                d = lax.rem(me + k, EH)

                @pl.when(d != me)
                def _():
                    text_copy(f, a, d).start()

                @pl.when(d == me)
                def _():
                    recv[f, a, me] = send_t[f, a, d]

        t = nn(s2mat[...], cols[f])
        send_i[f] = t.astype(BF16).reshape(EH, SL, FB)

        @pl.loop(0, EH)
        def _(k):
            d = lax.rem(me + k, EH)

            @pl.when(EH + d != me)
            def _():
                image_copy(f, d).start()

            @pl.when(EH + d == me)
            def _():
                recv[f, 0, me] = send_i[f, d]

    jq_row = jnp.floor((iota((1, NS), 1).astype(F32) + 0.5) * (1.0 / SL))
    jr_row = iota((1, NS), 1).astype(F32) - jq_row * SL
    jq_col = jnp.floor((iota((NS, 1), 0).astype(F32) + 0.5) * (1.0 / SL))
    jr_col = iota((NS, 1), 0).astype(F32) - jq_col * SL

    def source(p):
        return lax.shift_right_logical(p, 8).astype(F32)

    src_text = source(tpk[pl.ds(kcol, 1), :])
    src_image = jnp.concatenate(
        [source(ipk[pl.ds(kcol, 1), :]), jnp.full((1, TD - HALF), 99.0, F32)], axis=1)
    src = jnp.where(is_text, src_text, src_image)
    i16 = iota((NE, 1), 0).astype(F32)
    cnt16 = jnp.sum(one(src == i16), axis=1, keepdims=True)
    off16 = jnp.sum(one(src < i16), axis=1, keepdims=True)
    spread = iota((NE, NS), 0).astype(F32) == jq_row
    cnt_row = jnp.sum(jnp.where(spread, cnt16, 0.0), axis=0, keepdims=True)
    off_row = jnp.sum(jnp.where(spread, off16, 0.0), axis=0, keepdims=True)
    for a in range(2):
        shift = (lax.div(me, EH) * (SI * a)).astype(F32)
        place = jr_row - shift
        good = jnp.where((place >= 0.0) & (place < cnt_row), off_row + place, -1.0)
        pmat[a] = one(iota((TD, NS), 0).astype(F32) == good).astype(BF16)
    cnt_col = jnp.sum(one(src == jq_col), axis=1, keepdims=True)
    off_col = jnp.sum(one(src < jq_col), axis=1, keepdims=True)
    good_col = jnp.where(jr_col < cnt_col, off_col + jr_col, -1.0)
    ptmat[...] = one(iota((NS, TD), 1).astype(F32) == good_col).astype(BF16)

    st_t = nt(idn[...], st.astype(BF16)).astype(BF16)
    st_wide = nn(st_t, one(spread).astype(BF16))
    filled = st_wide == jr_row + 1.0
    omat[...] = one(filled).astype(BF16)
    k_row = jnp.where(jq_row >= EH, jq_row - EH, jq_row)
    spread_k = one(iota((EH, NS), 0).astype(F32) == k_row).astype(BF16)
    gate_wide = nn(gates[...], spread_k)
    gmat[...] = jnp.where(filled, gate_wide, 0.0).astype(BF16)
    vrecv[EH:, 32:, :] = jnp.zeros((EH, SL - 32, FB), BF16)
    srecv[h] = jnp.zeros((1, TD), F32)

    def y_copy(a, r, way):
        ref = x.at[a, y, rowsl(r), colsl(c)]
        return remote(ref, ref, sy.at[a, r, way], ry.at[a, r, way], hidden=(up, dn)[way] * 2 + c)

    def y_wait(a, r, way):
        ref = x.at[a, (dn, up)[way], rowsl(r), colsl(c)]
        remote(ref, ref, sy.at[a, r, way], ry.at[a, r, way], hidden=(dn, up)[way] * 2 + c).wait_recv()

    def core_copy(a, k, r):
        ref = x.at[a, blocks[k], rowsl(r), colsl(c)]
        return remote(ref, ref, sc.at[a, k, r], rc.at[a, k, r], hidden=y * 2 + oc)

    def core_wait(a, k, r):
        ref = x.at[a, blocks[k], rowsl(r), colsl(oc)]
        remote(ref, ref, sc.at[a, k, r], rc.at[a, k, r], hidden=y * 2 + oc).wait_recv()

    def compact(f, a):
        aa = a * (1 - lax.div(me, EH)) if a else 0

        def await_source(s):
            @pl.when(s != me)
            def _():
                remote(send_t.at[f, a, 0], recv.at[f, aa, s], s1t.at[f, a, 0], r1.at[f, aa, s], expert=s).wait_recv()

        if a == 0:
            pl.loop(0, NE)(await_source)
        else:
            @pl.when(is_text)
            def _():
                pl.loop(0, NE)(await_source)

        @pl.loop(0, n_chunks)
        def _(r):
            got = nn(pmat[a, rowsl(r), :], recv[f, aa].reshape(NS, FB))
            x[a, blocks[f], rowsl(r), colsl(c)] = got.astype(BF16)
            if f == 0:
                y_copy(a, r, 0).start()
                y_copy(a, r, 1).start()
            core_copy(a, f, r).start()

    def forward(a, k):
        @pl.loop(0, n_chunks)
        def _(r):
            y_wait(a, r, 1 if k == 2 else 0)
            core_copy(a, k, r).start()

    def project(a, k):
        yy = blocks[k]
        rows = pl.ds(pl.multiple_of(yy * YB, YB), YB)
        if a == 0:
            wloads[k][0].wait()
            wloads[k][1].wait()
        else:
            wloads[k][2].wait()

        @pl.loop(0, n_chunks)
        def _(r):
            core_wait(a, k, r)
            left = x[a, yy, rowsl(r), :]
            for n in range(FH // 256):
                ns = pl.ds(n * 256, 256)
                if a == 0:
                    outs = ((0, nn(left, wg[rows, ns])), (1, nn(left, wu[rows, ns])))
                else:
                    outs = ((2, nt(left, wd[ns, rows])),)
                for i, v in outs:
                    if k == 0:
                        acc[i, rowsl(r), ns] = v
                    else:
                        acc[i, rowsl(r), ns] += v

    compact(0, 0)
    compact(0, 1)
    project(0, 0)
    compact(1, 0)
    compact(1, 1)
    project(1, 0)
    forward(0, 2)
    forward(0, 3)
    project(0, 1)
    project(1, 1)
    forward(1, 2)
    forward(1, 3)
    project(0, 2)
    project(0, 3)
    project(1, 2)
    project(1, 3)

    keep = jnp.concatenate(
        [jnp.broadcast_to(mask[:, j:j + 1].astype(F32), (1, 128)) for j in range(8)], axis=1)
    eye = iota((128, 128), 0) == iota((128, 128), 1)

    @pl.loop(0, n_chunks * 2)
    def _(i):
        rows = pl.ds(pl.multiple_of(i * 128, 128), 128)
        gate_in = acc[0, rows, :]
        up_in = acc[1, rows, :]
        back = acc[2, rows, :]
        sig = jax.nn.sigmoid(gate_in)
        swish = gate_in * sig
        slope = sig * (1.0 + gate_in * (1.0 - sig))
        act = (swish * up_in * keep).astype(BF16).astype(F32)
        score = jnp.sum(act * back, axis=1, keepdims=True)
        hidden = back * keep
        gd[rows, :] = (hidden * up_in * slope).astype(BF16)
        ud[rows, :] = (hidden * swish).astype(BF16)
        srecv[h, :, pl.ds(pl.multiple_of(i * 128, 128), 128)] = jnp.sum(
            jnp.where(eye, score, 0.0), axis=0, keepdims=True)

    def score_copy(k):
        to = lax.rem(h + k, 8)
        return remote(srecv.at[h], srecv.at[h], ss.at[to], rs.at[h], hidden=to)

    @pl.loop(1, 8)
    def _(k):
        score_copy(k).start()

    order = (1, 2, 3, 0)

    def terms(j):
        yy = blocks[order[j]]

        @pl.loop(0, n_chunks)
        def _(r):
            gdr = gd[rowsl(r), :]
            udr = ud[rowsl(r), :]
            for n in range(YB // 256):
                ws = pl.ds(pl.multiple_of(yy * YB + n * 256, 256), 256)
                acc[j % 3, rowsl(r), n * 256:(n + 1) * 256] = nt(gdr, wg[ws, :]) + nt(udr, wu[ws, :])
            stage[j, rowsl(r), :] = acc[j % 3, rowsl(r), colsl(oc)].astype(BF16)
            pair_copy(j, r).start()

    def pair_copy(j, r):
        return remote(stage.at[j, rowsl(r), :], crecv.at[j, rowsl(r), :], scc.at[j, r], rcc.at[j, r],
                      hidden=y * 2 + oc)

    def half_copy(r, way):
        rows = pl.ds(pl.multiple_of(r * RC + way * 128, 128), 128)
        land = (arecv, brecv)[way]
        return remote(fstage.at[rows, :], land.at[r], sab.at[r, way], rab.at[r, way],
                      hidden=(up, dn)[way] * 2 + c)

    def full_copy(r, way):
        return remote((ustage, dstage)[way].at[rowsl(r), :], (urecv, drecv)[way].at[rowsl(r), :],
                      sud.at[r, way], rud.at[r, way], hidden=(up, dn)[way] * 2 + c)

    def pair_sum(j, r):
        pair_copy(j, r).wait_recv()
        return acc[j % 3, rowsl(r), colsl(c)] + crecv[j, rowsl(r), :].astype(F32)

    def finish(j):
        @pl.loop(0, n_chunks)
        def _(r):
            v = pair_sum(j, r)
            if j == 0:
                fstage[rowsl(r), :] = v.astype(BF16)
                half_copy(r, 0).start()
                half_copy(r, 1).start()
            elif j in (1, 2):
                way = j - 1
                half_copy(r, way).wait_recv()
                extra = (arecv, brecv)[way][r].astype(F32)
                zero = jnp.zeros_like(extra)
                pieces = [extra, zero] if way == 0 else [zero, extra]
                v = v + jnp.concatenate(pieces, axis=0)
                (ustage, dstage)[way][rowsl(r), :] = v.astype(BF16)
                full_copy(r, way).start()
            else:
                full_copy(r, 0).wait_recv()
                full_copy(r, 1).wait_recv()
                v = v + urecv[rowsl(r), :].astype(F32) + drecv[rowsl(r), :].astype(F32)
                rgm[rowsl(r), :] = v.astype(BF16)

    terms(0)
    terms(1)
    finish(0)
    terms(2)
    finish(1)
    terms(3)
    finish(2)

    def slot_copy(d):
        return remote(scs.at[d], scr.at[me], sq.at[d], rq.at[me], expert=d)

    @pl.loop(1, 8)
    def _(k):
        frm = lax.rem(h + k, 8)
        remote(srecv.at[h], srecv.at[frm], ss.at[frm], rs.at[frm], hidden=frm).wait_recv()

    total = srecv[0]
    for k in range(1, 8):
        total = total + srecv[k]
    total = total.astype(BF16).astype(F32)
    for part in range(4):
        rows = pl.ds(part * (NS // 4), NS // 4)
        scol = jnp.sum(ptmat[rows, :].astype(F32) * total, axis=1, keepdims=True)
        put = jnp.where(iota((NS // 4, 128), 1) == kcol, scol, 0.0).astype(BF16)
        scs[pl.ds(part * 4, 4)] = put.reshape(4, SL, 128)

    @pl.loop(1, NE)
    def _(k):
        slot_copy(lax.rem(me + k, NE)).start()

    scr[me] = scs[me]

    finish(3)

    @pl.when(jnp.logical_not(is_text))
    def _():
        rgm[RC:, :] = jnp.zeros((TD - RC, FB), BF16)

    vsend[...] = nn(ptmat[...], rgm[...]).astype(BF16).reshape(NE, SL, FB)

    def row_copy(d, n):
        return remote(vsend.at[d, pl.ds(0, n), :], vrecv.at[me, pl.ds(0, n), :], sv.at[d], rv.at[me], expert=d)

    def row_wait(s, n):
        remote(vsend.at[s, pl.ds(0, n), :], vrecv.at[s, pl.ds(0, n), :], sv.at[s], rv.at[s], expert=s).wait_recv()

    @pl.when(is_text)
    def _():
        @pl.loop(1, NE)
        def _(k):
            row_copy(lax.rem(me + k, NE), SL).start()

    @pl.when(jnp.logical_not(is_text))
    def _():
        @pl.loop(1, NE)
        def _(k):
            row_copy(lax.rem(me + k, NE), 32).start()

    vrecv[me, :32, :] = vsend[me, :32, :]

    @pl.when(is_text)
    def _():
        vrecv[me, 32:, :] = vsend[me, 32:, :]

    @pl.loop(0, NE)
    def _(s):
        @pl.when(s != me)
        def _():
            remote(scs.at[s], scr.at[s], sq.at[s], rq.at[s], expert=s).wait_recv()

    rg[...] = nn(omat[...], scr[...].reshape(NS, 128))[:, :EH].astype(BF16)

    @pl.loop(0, EH)
    def _(s):
        @pl.when(s != me)
        def _():
            row_wait(s, SL)

    @pl.loop(EH, NE)
    def _(s):
        @pl.when(s != me)
        def _():
            row_wait(s, 32)

    ig[...] = nn(gmat[...], vrecv[...].reshape(NS, FB)).astype(BF16)

    for f in range(2):
        @pl.loop(0, EH)
        def _(d):
            @pl.when(d != me)
            def _():
                text_copy(f, 0, d).wait_send()
                text_copy(f, 1, d).wait_send()

            @pl.when(EH + d != me)
            def _():
                image_copy(f, d).wait_send()

    @pl.loop(0, n_chunks)
    def _(r):
        for a in range(2):
            y_copy(a, r, 0).wait_send()
            y_copy(a, r, 1).wait_send()
            for k in range(4):
                core_copy(a, k, r).wait_send()
        for j in range(4):
            pair_copy(j, r).wait_send()
        for way in range(2):
            half_copy(r, way).wait_send()
            full_copy(r, way).wait_send()

    @pl.loop(1, 8)
    def _(k):
        score_copy(k).wait_send()

    @pl.loop(1, NE)
    def _(k):
        slot_copy(lax.rem(me + k, NE)).wait_send()

    @pl.when(is_text)
    def _():
        @pl.loop(1, NE)
        def _(k):
            row_copy(lax.rem(me + k, NE), SL).wait_send()

    @pl.when(jnp.logical_not(is_text))
    def _():
        @pl.loop(1, NE)
        def _(k):
            row_copy(lax.rem(me + k, NE), 32).wait_send()


def body(tokens, out_grad, gates, labels, text_picks, image_picks, block_mask, w_gate, w_up, w_down):
    any_spec = pl.BlockSpec(memory_space=pl.ANY)
    vmem = pl.BlockSpec(memory_space=pltpu.VMEM)
    dma = pltpu.SemaphoreType.DMA
    return pl.pallas_call(
        kernel,
        out_shape=(
            jax.ShapeDtypeStruct((TD, FB), BF16),
            jax.ShapeDtypeStruct((TD, EH), BF16),
        ),
        in_specs=[any_spec, any_spec, vmem, vmem, vmem, vmem, vmem, any_spec, any_spec, any_spec],
        out_specs=(vmem, vmem),
        scratch_shapes=[
            pltpu.VMEM((D, FH), BF16),
            pltpu.VMEM((D, FH), BF16),
            pltpu.VMEM((FH, D), BF16),
            pltpu.VMEM((2, 2 * TD, FB), BF16),
            pltpu.VMEM((TD, TD), BF16),
            pltpu.VMEM((TD, TD), BF16),
            pltpu.VMEM((NE, HALF), F32),
            pltpu.VMEM((EH * SL, TD), BF16),
            pltpu.VMEM((EH * SL, 2 * TD), BF16),
            pltpu.VMEM((TD, NS), BF16),
            pltpu.VMEM((TD, NS), BF16),
            pltpu.VMEM((2, TD, NS), BF16),
            pltpu.VMEM((NS, TD), BF16),
            pltpu.VMEM((2, 2, EH, SL, FB), BF16),
            pltpu.VMEM((2, EH, SL, FB), BF16),
            pltpu.VMEM((2, 2, NE, SL, FB), BF16),
            pltpu.VMEM((2, 4, TD, YB), BF16),
            pltpu.VMEM((3, TD, FH), F32),
            pltpu.VMEM((TD, FH), BF16),
            pltpu.VMEM((TD, FH), BF16),
            pltpu.VMEM((4, TD, FB), BF16),
            pltpu.VMEM((4, TD, FB), BF16),
            pltpu.VMEM((TD, FB), BF16),
            pltpu.VMEM((TD, FB), BF16),
            pltpu.VMEM((TD, FB), BF16),
            pltpu.VMEM((2, 128, FB), BF16),
            pltpu.VMEM((2, 128, FB), BF16),
            pltpu.VMEM((TD, FB), BF16),
            pltpu.VMEM((TD, FB), BF16),
            pltpu.VMEM((TD, FB), BF16),
            pltpu.VMEM((NE, SL, FB), BF16),
            pltpu.VMEM((NE, SL, FB), BF16),
            pltpu.VMEM((8, 1, TD), F32),
            pltpu.VMEM((NE, SL, 128), BF16),
            pltpu.VMEM((NE, SL, 128), BF16),
            dma((2, 2)),
            dma((4, 3)),
            dma((2, 2, EH)),
            dma((2, EH)),
            dma((2, 2, NE)),
            dma((2, 2, 2)),
            dma((2, 2, 2)),
            dma((2, 4, 2)),
            dma((2, 4, 2)),
            dma((8,)),
            dma((8,)),
            dma((4, 2)),
            dma((4, 2)),
            dma((2, 2)),
            dma((2, 2)),
            dma((2, 2)),
            dma((2, 2)),
            dma((NE,)),
            dma((NE,)),
            dma((NE,)),
            dma((NE,)),
        ],
        compiler_params=pltpu.CompilerParams(
            collective_id=0, has_side_effects=True, vmem_limit_bytes=62 * 1024 * 1024),
        cost_estimate=pl.CostEstimate(flops=16_000_000_000, bytes_accessed=22_000_000, transcendentals=1_000_000),
    )(
        tokens, out_grad, gates, labels.reshape(1, TD), text_picks, image_picks, block_mask,
        w_gate[0], w_up[0], w_down[0],
    )


def solution(mesh):
    placed = (
        P("expert", None),
        P("expert", None),
        P("expert", None),
        P("expert"),
        P(),
        P(),
        P("expert", "hidden"),
        P("expert", None, "hidden"),
        P("expert", None, "hidden"),
        P("expert", "hidden", None),
    )
    return jax.shard_map(
        body,
        mesh=mesh,
        in_specs=placed,
        out_specs=(P("expert", "hidden"), P("expert", None)),
        check_vma=False,
    )
```

```python
import jax
import jax.numpy as jnp
from jax import lax
from jax.experimental import pallas as pl
from jax.experimental.pallas import tpu as pltpu
from jax.sharding import PartitionSpec as P

MESH = pl.DeviceIdType.MESH
F32 = jnp.float32
BF16 = jnp.bfloat16

TD = 512
HALF = 256
NE = 16
EH = 8
SL = 48
SI = 24
NS = NE * SL
D = 3072
FB = 384
YB = 768
FH = 1024
RC = 256
PART = (0, 256, 384)


def nt(a, b):
    return lax.dot_general(a, b, (((1,), (1,)), ((), ())), preferred_element_type=F32)


def nn(a, b):
    return jnp.dot(a, b, preferred_element_type=F32)


def iota(shape, dim):
    return lax.broadcasted_iota(jnp.int32, shape, dim)


def one(cond):
    return jnp.where(cond, 1.0, 0.0).astype(F32)


def kernel(
    tok_h, og_h, gates, labels, tpk, ipk, mask, wg_h, wu_h, wd_h,
    ig, rg,
    wg, wu, wd, cols, tri, idn, mref, smat, s2mat, gmat, omat, pmat, ptmat,
    send_t, send_i, recv, x, acc, gd, ud, stage, crecv, fstage, ustage, dstage,
    arecv, brecv, urecv, drecv, rgm, vsend, vrecv, ssend, sland, srecv,
    ld_sem, w_sem, s1t, s1i, r1, sy, ry, sc, rc, ss, rs, scc, rcc, sab, rab, sud, rud,
    sv, rv,
):
    me = lax.axis_index("expert")
    h = lax.axis_index("hidden")
    y = lax.div(h, 2)
    c = lax.rem(h, 2)
    oc = 1 - c
    far = lax.rem(y + 2, 4)
    up = lax.rem(y + 1, 4)
    dn = lax.rem(y + 3, 4)
    kcol = lax.rem(me, EH)
    is_text = me < EH
    n_chunks = 2 - lax.div(me, EH)
    blocks = (y, far, up, dn)

    def remote(src, dst, s_sem, r_sem, **where):
        return pltpu.make_async_remote_copy(
            src_ref=src, dst_ref=dst, send_sem=s_sem, recv_sem=r_sem,
            device_id=where, device_id_type=MESH,
        )

    def colsl(core):
        return pl.ds(pl.multiple_of(core * FB, 128), FB)

    def rowsl(r):
        return pl.ds(pl.multiple_of(r * RC, RC), RC)

    leave = []
    text_gone = {}

    def both(rows_of):
        @pl.when(is_text)
        def _():
            rows_of(TD)

        @pl.when(jnp.logical_not(is_text))
        def _():
            rows_of(RC)

    loads = []
    for f, yy in enumerate((y, far)):
        fs = pl.ds(pl.multiple_of((yy * 2 + c) * FB, 128), FB)
        for a, src in enumerate((tok_h, og_h)):
            cp = pltpu.make_async_copy(
                src.at[:, fs], cols.at[f, pl.ds(a * TD, TD), :], ld_sem.at[f, a])
            cp.start()
            loads.append(cp)
    wloads = []
    for k, yy in enumerate(blocks):
        rows = pl.ds(pl.multiple_of(yy * YB, YB), YB)
        trio = [
            pltpu.make_async_copy(wg_h.at[rows, :], wg.at[rows, :], w_sem.at[k, 0]),
            pltpu.make_async_copy(wu_h.at[rows, :], wu.at[rows, :], w_sem.at[k, 1]),
            pltpu.make_async_copy(wd_h.at[:, rows], wd.at[:, rows], w_sem.at[k, 2]),
        ]
        for cp in trio:
            cp.start()
        wloads.append(trio)

    barrier = pltpu.get_barrier_semaphore()

    @pl.loop(1, NE)
    def _(k):
        pl.semaphore_signal(barrier, inc=1, device_id={"expert": lax.rem(me + k, NE)}, device_id_type=MESH)

    @pl.loop(1, 8)
    def _(k):
        pl.semaphore_signal(barrier, inc=1, device_id={"hidden": lax.rem(h + k, 8)}, device_id_type=MESH)

    r5 = iota((TD, TD), 0)
    c5 = iota((TD, TD), 1)
    tri[...] = one(r5 <= c5).astype(BF16)
    idn[...] = one(r5 == c5).astype(BF16)
    text = one(labels[...] == 0)
    lab16 = jnp.where(iota((NE, TD), 0) < EH, text, 1.0 - text)
    rank = nn(lab16.astype(BF16), tri[...])
    key = jnp.where(lab16 > 0.0, rank - 1.0, -1.0)

    def local_rank(p):
        return jnp.where(lax.shift_right_logical(p, 8) == me, (p & 255), -1).astype(F32)

    lov = jnp.concatenate([
        local_rank(tpk[...]),
        jnp.concatenate([local_rank(ipk[...]), jnp.full((EH, TD - HALF), -1.0, F32)], axis=1),
    ], axis=0)
    lov_t = nt(idn[...], lov.astype(BF16))
    rrow = iota((1, HALF), 1).astype(F32)
    def slots(e0, depth):
        for e in range(e0, e0 + EH):
            hit = one(lov_t[:depth, e:e + 1] == rrow)
            mref[e:e + 1, :] = jnp.sum(hit, axis=0, keepdims=True)
        member = mref[e0:e0 + EH, :]
        slot = member * nn(member.astype(BF16), tri[:HALF, :HALF])
        rcol = iota((HALF, TD), 0).astype(F32)
        return nn(slot.astype(BF16), one(rcol == key[e0:e0 + 1, :]).astype(BF16))

    st_text = slots(0, TD)
    s1 = iota((SL, TD), 0).astype(F32) + 1.0
    for e in range(EH):
        smat[e * SL:(e + 1) * SL, :] = one(st_text[e:e + 1, :] == s1).astype(BF16)

    pl.semaphore_wait(barrier, NE - 1 + 7)

    def text_copy(f, a, d):
        return remote(send_t.at[f, a, d], recv.at[f, a, me], s1t.at[f, a, d], r1.at[f, a, me], expert=d)

    def image_copy(f, d):
        return remote(send_i.at[f, d], recv.at[f, 0, me], s1i.at[f, d], r1.at[f, 0, me], expert=EH + d)

    def pick_text(f, a):
        loads[f * 2 + a].wait()
        t = nn(smat[...], cols[f, a * TD:(a + 1) * TD, :])
        send_t[f, a] = t.astype(BF16).reshape(EH, SL, FB)

        @pl.loop(0, EH)
        def _(k):
            d = lax.rem(me + k, EH)

            @pl.when(d != me)
            def _():
                text_copy(f, a, d).start()

            @pl.when(d == me)
            def _():
                recv[f, a, me] = send_t[f, a, d]

        def gone():
            @pl.loop(0, EH)
            def _(d):
                @pl.when(d != me)
                def _():
                    text_copy(f, a, d).wait_send()

        text_gone[f, a] = gone

    def left(f, a):
        text_gone.pop((f, a))()

    def pick_image(f):
        t = nn(s2mat[...], cols[f])
        send_i[f] = t.astype(BF16).reshape(EH, SL, FB)

        @pl.loop(0, EH)
        def _(k):
            d = lax.rem(me + k, EH)

            @pl.when(EH + d != me)
            def _():
                image_copy(f, d).start()

            @pl.when(EH + d == me)
            def _():
                recv[f, 0, me] = send_i[f, d]

        @leave.append
        def _():
            @pl.loop(0, EH)
            def _(d):
                @pl.when(EH + d != me)
                def _():
                    image_copy(f, d).wait_send()

    pick_text(0, 0)

    st_image = slots(EH, HALF)
    for e in range(EH):
        im = st_image[e:e + 1, :]
        s2mat[e * SL:(e + 1) * SL, :TD] = one(im == s1).astype(BF16)
        im2 = jnp.where(im > 0.0, im + SI, -1.0)
        s2mat[e * SL:(e + 1) * SL, TD:] = one(im2 == s1).astype(BF16)

    jq_row = jnp.floor((iota((1, NS), 1).astype(F32) + 0.5) * (1.0 / SL))
    jr_row = iota((1, NS), 1).astype(F32) - jq_row * SL
    jq_col = jnp.floor((iota((NS, 1), 0).astype(F32) + 0.5) * (1.0 / SL))
    jr_col = iota((NS, 1), 0).astype(F32) - jq_col * SL

    def source(p):
        return lax.shift_right_logical(p, 8).astype(F32)

    src_text = source(tpk[pl.ds(kcol, 1), :])
    src_image = jnp.concatenate(
        [source(ipk[pl.ds(kcol, 1), :]), jnp.full((1, TD - HALF), 99.0, F32)], axis=1)
    src = jnp.where(is_text, src_text, src_image)
    i16 = iota((NE, 1), 0).astype(F32)
    cnt16 = jnp.sum(one(src == i16), axis=1, keepdims=True)
    off16 = jnp.sum(one(src < i16), axis=1, keepdims=True)
    spread = iota((NE, NS), 0).astype(F32) == jq_row
    cnt_row = jnp.sum(jnp.where(spread, cnt16, 0.0), axis=0, keepdims=True)
    off_row = jnp.sum(jnp.where(spread, off16, 0.0), axis=0, keepdims=True)
    for a in range(2):
        shift = (lax.div(me, EH) * (SI * a)).astype(F32)
        place = jr_row - shift
        good = jnp.where((place >= 0.0) & (place < cnt_row), off_row + place, -1.0)
        pmat[a] = one(iota((TD, NS), 0).astype(F32) == good).astype(BF16)
    cnt_col = jnp.sum(one(src == jq_col), axis=1, keepdims=True)
    off_col = jnp.sum(one(src < jq_col), axis=1, keepdims=True)
    good_col = jnp.where(jr_col < cnt_col, off_col + jr_col, -1.0)
    ptmat[...] = one(iota((NS, TD), 1).astype(F32) == good_col).astype(BF16)

    def owner_tables():
        st = jnp.concatenate([st_text, st_image], axis=0)
        st_t = nt(idn[...], st.astype(BF16)).astype(BF16)
        st_wide = nn(st_t, one(spread).astype(BF16))
        filled = st_wide == jr_row + 1.0
        omat[...] = one(filled).astype(BF16)
        k_row = jnp.where(jq_row >= EH, jq_row - EH, jq_row)
        spread_k = one(iota((EH, NS), 0).astype(F32) == k_row).astype(BF16)
        gate_wide = nn(nt(idn[...], gates[...]).astype(BF16), spread_k)
        gmat[...] = jnp.where(filled, gate_wide, 0.0).astype(BF16)

    vrecv[EH:, 32:, :] = jnp.zeros((EH, SL - 32, FB), BF16)
    sland[EH:, 32:, :] = jnp.zeros((EH, SL - 32, 128), BF16)

    @pl.when(jnp.logical_not(is_text))
    def _():
        rgm[RC:, :] = jnp.zeros((TD - RC, FB), BF16)

    srecv[h] = jnp.zeros((1, TD), F32)

    def y_copy(a, r, way):
        ref = x.at[a, y, rowsl(r), colsl(c)]
        return remote(ref, ref, sy.at[a, r, way], ry.at[a, r, way], hidden=(up, dn)[way] * 2 + c)

    def y_wait(a, r, way):
        ref = x.at[a, (dn, up)[way], rowsl(r), colsl(c)]
        remote(ref, ref, sy.at[a, r, way], ry.at[a, r, way], hidden=(dn, up)[way] * 2 + c).wait_recv()

    def core_copy(a, k, r):
        ref = x.at[a, blocks[k], rowsl(r), colsl(c)]
        return remote(ref, ref, sc.at[a, k, r], rc.at[a, k, r], hidden=y * 2 + oc)

    def core_wait(a, k, r):
        ref = x.at[a, blocks[k], rowsl(r), colsl(oc)]
        remote(ref, ref, sc.at[a, k, r], rc.at[a, k, r], hidden=y * 2 + oc).wait_recv()

    def chunks_left(*copies, only=None):
        def wait():
            @pl.loop(0, n_chunks)
            def _(r):
                for copy in copies:
                    copy(r).wait_send()

        leave.append(wait if only is None else lambda: pl.when(only)(wait))

    def compact(f, a, text_expert):
        aa = a if text_expert else 0

        @pl.when(is_text if text_expert else jnp.logical_not(is_text))
        def _():
            if text_expert or a == 0:
                @pl.loop(0, NE)
                def _(s):
                    @pl.when(s != me)
                    def _():
                        remote(send_t.at[f, a, 0], recv.at[f, aa, s], s1t.at[f, a, 0], r1.at[f, aa, s],
                               expert=s).wait_recv()

            @pl.loop(0, 2 if text_expert else 1)
            def _(r):
                got = nn(pmat[a, rowsl(r), :], recv[f, aa].reshape(NS, FB))
                x[a, blocks[f], rowsl(r), colsl(c)] = got.astype(BF16)
                if f == 0:
                    y_copy(a, r, 0).start()
                    y_copy(a, r, 1).start()
                core_copy(a, f, r).start()

        copies = [lambda r: core_copy(a, f, r)]
        if f == 0:
            copies += [lambda r: y_copy(a, r, 0), lambda r: y_copy(a, r, 1)]
        chunks_left(*copies, only=is_text if text_expert else jnp.logical_not(is_text))

    def forward(a, k):
        @pl.loop(0, n_chunks)
        def _(r):
            y_wait(a, r, 1 if k == 2 else 0)
            core_copy(a, k, r).start()

        chunks_left(lambda r: core_copy(a, k, r))

    def project(a, k):
        yy = blocks[k]
        rows = pl.ds(pl.multiple_of(yy * YB, YB), YB)
        if a == 0:
            wloads[k][0].wait()
            wloads[k][1].wait()
        else:
            wloads[k][2].wait()

        @pl.loop(0, n_chunks)
        def _(r):
            core_wait(a, k, r)

        def rows_of(m):
            left = x[a, yy, :m, :]
            for n in range(FH // 256):
                ns = pl.ds(n * 256, 256)
                if a == 0:
                    outs = ((0, nn(left, wg[rows, ns])), (1, nn(left, wu[rows, ns])))
                else:
                    outs = ((2, nt(left, wd[ns, rows])),)
                for i, v in outs:
                    if k == 0:
                        acc[i, :m, ns] = v
                    else:
                        acc[i, :m, ns] += v

        both(rows_of)

    pick_text(0, 1)
    pick_image(0)
    left(0, 0)
    pick_text(1, 0)
    compact(0, 0, True)
    left(0, 1)
    pick_text(1, 1)
    pick_image(1)
    compact(0, 1, True)
    compact(0, 0, False)
    compact(0, 1, False)
    owner_tables()
    project(0, 0)
    forward(0, 2)
    forward(0, 3)
    compact(1, 0, True)
    project(1, 0)
    project(0, 2)
    project(0, 3)
    compact(1, 0, False)
    compact(1, 1, False)
    compact(1, 1, True)
    project(0, 1)
    forward(1, 2)
    forward(1, 3)
    project(1, 1)
    project(1, 2)
    project(1, 3)

    keep = jnp.concatenate(
        [jnp.broadcast_to(mask[:, j:j + 1].astype(F32), (1, 128)) for j in range(8)], axis=1)
    eye = iota((128, 128), 0) == iota((128, 128), 1)

    @pl.loop(0, n_chunks * 2)
    def _(i):
        rows = pl.ds(pl.multiple_of(i * 128, 128), 128)
        gate_in = acc[0, rows, :]
        up_in = acc[1, rows, :]
        back = acc[2, rows, :]
        sig = jax.nn.sigmoid(gate_in)
        swish = gate_in * sig
        slope = sig * (1.0 + gate_in * (1.0 - sig))
        act = (swish * up_in * keep).astype(BF16).astype(F32)
        score = jnp.sum(act * back, axis=1, keepdims=True)
        hidden = back * keep
        gd[rows, :] = (hidden * up_in * slope).astype(BF16)
        ud[rows, :] = (hidden * swish).astype(BF16)
        srecv[h, :, pl.ds(pl.multiple_of(i * 128, 128), 128)] = jnp.sum(
            jnp.where(eye, score, 0.0), axis=0, keepdims=True)

    def score_copy(k):
        to = lax.rem(h + k, 8)
        return remote(srecv.at[h], srecv.at[h], ss.at[to], rs.at[h], hidden=to)

    @pl.loop(1, 8)
    def _(k):
        score_copy(k).start()

    @leave.append
    def _():
        @pl.loop(1, 8)
        def _(k):
            score_copy(k).wait_send()

    order = (1, 2, 3, 0)

    def part(s):
        return slice(PART[s], PART[s + 1])

    def kept(s, j):
        return j // 2, slice(j % 2 * FB + PART[s], j % 2 * FB + PART[s + 1])

    def pair_copy(s, j, n):
        ref = stage.at[j, pl.ds(0, n), part(s)], crecv.at[j, pl.ds(0, n), part(s)]
        return remote(*ref, scc.at[s, j], rcc.at[s, j], hidden=y * 2 + oc)

    def half(way, n):
        return pl.ds(way * (n // 2), n // 2)

    def half_copy(s, way, n):
        land = (arecv, brecv)[way]
        return remote(fstage.at[half(way, n), part(s)], land.at[pl.ds(0, n // 2), part(s)],
                      sab.at[s, way], rab.at[s, way], hidden=(up, dn)[way] * 2 + c)

    def full_copy(s, way, m, n):
        return remote((ustage, dstage)[way].at[half(m, n), part(s)], (urecv, drecv)[way].at[half(m, n), part(s)],
                      sud.at[s, way, m], rud.at[s, way, m], hidden=(up, dn)[way] * 2 + c)

    def later(copy):
        leave.append(lambda: both(lambda n: copy(n).wait_send()))

    def terms(s, j):
        wide = PART[s + 1] - PART[s]
        base = blocks[order[j]] * YB + PART[s]
        mine = pl.ds(pl.multiple_of(base + c * FB, 128), wide)
        other = pl.ds(pl.multiple_of(base + oc * FB, 128), wide)
        at, lanes = kept(s, j)

        def rows_of(n):
            wgs = jnp.concatenate([wg[mine, :], wg[other, :]], axis=0)
            wus = jnp.concatenate([wu[mine, :], wu[other, :]], axis=0)
            v = nt(gd[:n, :], wgs) + nt(ud[:n, :], wus)
            stage[j, :n, part(s)] = v[:, wide:].astype(BF16)
            pair_copy(s, j, n).start()
            acc[at, :n, lanes] = v[:, :wide]

        both(rows_of)
        later(lambda n: pair_copy(s, j, n))

    def pair_sum(s, j, m, n):
        at, lanes = kept(s, j)
        return acc[at, half(m, n), lanes] + crecv[j, half(m, n), part(s)].astype(F32)

    def finish_far(s):
        def rows_of(n):
            pair_copy(s, 0, n).wait_recv()
            for way in range(2):
                fstage[half(way, n), part(s)] = pair_sum(s, 0, way, n).astype(BF16)
                half_copy(s, way, n).start()

        both(rows_of)
        later(lambda n: half_copy(s, 0, n))
        later(lambda n: half_copy(s, 1, n))

    def finish_free(s, way):
        def rows_of(n):
            pair_copy(s, 1 + way, n).wait_recv()
            (ustage, dstage)[way][half(1 - way, n), part(s)] = pair_sum(s, 1 + way, 1 - way, n).astype(BF16)
            full_copy(s, way, 1 - way, n).start()

        both(rows_of)
        later(lambda n: full_copy(s, way, 1 - way, n))

    def finish_rest(s, way):
        def rows_of(n):
            half_copy(s, way, n).wait_recv()
            v = pair_sum(s, 1 + way, way, n) + (arecv, brecv)[way][:n // 2, part(s)].astype(F32)
            (ustage, dstage)[way][half(way, n), part(s)] = v.astype(BF16)
            full_copy(s, way, way, n).start()

        both(rows_of)
        later(lambda n: full_copy(s, way, way, n))

    def finish_own(s):
        def rows_of(n):
            pair_copy(s, 3, n).wait_recv()
            for m in (1, 0):
                full_copy(s, 0, m, n).wait_recv()
                full_copy(s, 1, m, n).wait_recv()
                v = pair_sum(s, 3, m, n)
                v = v + urecv[half(m, n), part(s)].astype(F32) + drecv[half(m, n), part(s)].astype(F32)
                rgm[half(m, n), part(s)] = v.astype(BF16)

        both(rows_of)

    def row_copy(p, d, n):
        if p == len(PART) - 1:
            src, dst = ssend.at[d, pl.ds(0, n), :], sland.at[me, pl.ds(0, n), :]
        else:
            src, dst = vsend.at[d, pl.ds(0, n), part(p)], vrecv.at[me, pl.ds(0, n), part(p)]
        return remote(src, dst, sv.at[p, d], rv.at[p, me], expert=d)

    def row_wait(p, n, first, last):
        @pl.loop(first, last)
        def _(s):
            @pl.when(s != me)
            def _():
                if p == len(PART) - 1:
                    src, dst = ssend.at[s, pl.ds(0, n), :], sland.at[s, pl.ds(0, n), :]
                else:
                    src, dst = vsend.at[s, pl.ds(0, n), part(p)], vrecv.at[s, pl.ds(0, n), part(p)]
                remote(src, dst, sv.at[p, s], rv.at[p, s], expert=s).wait_recv()

    def row_send(p):
        def all_rows(act):
            @pl.when(is_text)
            def _():
                @pl.loop(1, NE)
                def _(k):
                    act(row_copy(p, lax.rem(me + k, NE), SL))

            @pl.when(jnp.logical_not(is_text))
            def _():
                @pl.loop(1, NE)
                def _(k):
                    act(row_copy(p, lax.rem(me + k, NE), 32))

        all_rows(lambda copy: copy.start())
        src, dst, lanes = (ssend, sland, slice(None)) if p == len(PART) - 1 else (vsend, vrecv, part(p))
        dst[me, :32, lanes] = src[me, :32, lanes]

        @pl.when(is_text)
        def _():
            dst[me, 32:, lanes] = src[me, 32:, lanes]

        leave.append(lambda: all_rows(lambda copy: copy.wait_send()))

    def send_scores():
        @pl.loop(1, 8)
        def _(k):
            frm = lax.rem(h + k, 8)
            remote(srecv.at[h], srecv.at[frm], ss.at[frm], rs.at[frm], hidden=frm).wait_recv()

        total = srecv[0]
        for k in range(1, 8):
            total = total + srecv[k]
        total = total.astype(BF16).astype(F32)
        for q in range(4):
            rows = pl.ds(q * (NS // 4), NS // 4)
            scol = jnp.sum(ptmat[rows, :].astype(F32) * total, axis=1, keepdims=True)
            put = jnp.where(iota((NS // 4, 128), 1) == kcol, scol, 0.0).astype(BF16)
            ssend[pl.ds(q * 4, 4)] = put.reshape(4, SL, 128)
        row_send(len(PART) - 1)

    def send_rows(s):
        finish_own(s)
        wide = PART[s + 1] - PART[s]
        vsend[:, :, part(s)] = nn(ptmat[...], rgm[:, part(s)]).astype(BF16).reshape(NE, SL, wide)
        row_send(s)

    def scores_here():
        row_wait(len(PART) - 1, SL, 0, EH)
        row_wait(len(PART) - 1, 32, EH, NE)
        rg[...] = jnp.transpose(nn(omat[...], sland[...].reshape(NS, 128)))[:EH].astype(BF16)

    def rows_here(s):
        row_wait(s, SL, 0, EH)
        row_wait(s, 32, EH, NE)
        wide = PART[s + 1] - PART[s]
        ig[:, part(s)] = nn(gmat[...], vrecv[:, :, part(s)].reshape(NS, wide)).astype(BF16)

    def flush():
        for wait in leave + list(text_gone.values()):
            wait()
        leave.clear()
        text_gone.clear()

    terms(0, 0)
    terms(0, 1)
    finish_far(0)
    terms(0, 2)
    finish_free(0, 0)
    terms(0, 3)
    finish_free(0, 1)
    terms(1, 0)
    finish_rest(0, 0)
    finish_rest(0, 1)
    terms(1, 1)
    finish_far(1)
    terms(1, 2)
    finish_free(1, 0)
    terms(1, 3)
    finish_free(1, 1)
    send_scores()
    finish_rest(1, 0)
    finish_rest(1, 1)
    send_rows(0)
    flush()
    send_rows(1)
    scores_here()
    rows_here(0)
    rows_here(1)

    flush()


def body(tokens, out_grad, gates, labels, text_picks, image_picks, block_mask, w_gate, w_up, w_down):
    any_spec = pl.BlockSpec(memory_space=pl.ANY)
    vmem = pl.BlockSpec(memory_space=pltpu.VMEM)
    dma = pltpu.SemaphoreType.DMA
    input_grad, router_grad = pl.pallas_call(
        kernel,
        out_shape=(
            jax.ShapeDtypeStruct((TD, FB), BF16),
            jax.ShapeDtypeStruct((EH, TD), BF16),
        ),
        in_specs=[any_spec, any_spec, vmem, vmem, vmem, vmem, vmem, any_spec, any_spec, any_spec],
        out_specs=(vmem, vmem),
        scratch_shapes=[
            pltpu.VMEM((D, FH), BF16),
            pltpu.VMEM((D, FH), BF16),
            pltpu.VMEM((FH, D), BF16),
            pltpu.VMEM((2, 2 * TD, FB), BF16),
            pltpu.VMEM((TD, TD), BF16),
            pltpu.VMEM((TD, TD), BF16),
            pltpu.VMEM((NE, HALF), F32),
            pltpu.VMEM((EH * SL, TD), BF16),
            pltpu.VMEM((EH * SL, 2 * TD), BF16),
            pltpu.VMEM((TD, NS), BF16),
            pltpu.VMEM((TD, NS), BF16),
            pltpu.VMEM((2, TD, NS), BF16),
            pltpu.VMEM((NS, TD), BF16),
            pltpu.VMEM((2, 2, EH, SL, FB), BF16),
            pltpu.VMEM((2, EH, SL, FB), BF16),
            pltpu.VMEM((2, 2, NE, SL, FB), BF16),
            pltpu.VMEM((2, 4, TD, YB), BF16),
            pltpu.VMEM((3, TD, FH), F32),
            pltpu.VMEM((TD, FH), BF16),
            pltpu.VMEM((TD, FH), BF16),
            pltpu.VMEM((4, TD, FB), BF16),
            pltpu.VMEM((4, TD, FB), BF16),
            pltpu.VMEM((TD, FB), BF16),
            pltpu.VMEM((TD, FB), BF16),
            pltpu.VMEM((TD, FB), BF16),
            pltpu.VMEM((TD // 2, FB), BF16),
            pltpu.VMEM((TD // 2, FB), BF16),
            pltpu.VMEM((TD, FB), BF16),
            pltpu.VMEM((TD, FB), BF16),
            pltpu.VMEM((TD, FB), BF16),
            pltpu.VMEM((NE, SL, FB), BF16),
            pltpu.VMEM((NE, SL, FB), BF16),
            pltpu.VMEM((NE, SL, 128), BF16),
            pltpu.VMEM((NE, SL, 128), BF16),
            pltpu.VMEM((8, 1, TD), F32),
            dma((2, 2)),
            dma((4, 3)),
            dma((2, 2, EH)),
            dma((2, EH)),
            dma((2, 2, NE)),
            dma((2, 2, 2)),
            dma((2, 2, 2)),
            dma((2, 4, 2)),
            dma((2, 4, 2)),
            dma((8,)),
            dma((8,)),
            dma((2, 4)),
            dma((2, 4)),
            dma((2, 2)),
            dma((2, 2)),
            dma((2, 2, 2)),
            dma((2, 2, 2)),
            dma((3, NE)),
            dma((3, NE)),
        ],
        compiler_params=pltpu.CompilerParams(
            collective_id=0, has_side_effects=True, vmem_limit_bytes=62 * 1024 * 1024),
        cost_estimate=pl.CostEstimate(flops=16_000_000_000, bytes_accessed=22_000_000, transcendentals=1_000_000),
    )(
        tokens, out_grad, gates.T, labels.reshape(1, TD), text_picks, image_picks, block_mask,
        w_gate[0], w_up[0], w_down[0],
    )
    return input_grad, router_grad.T


def solution(mesh):
    placed = (
        P("expert", None),
        P("expert", None),
        P("expert", None),
        P("expert"),
        P(),
        P(),
        P("expert", "hidden"),
        P("expert", None, "hidden"),
        P("expert", None, "hidden"),
        P("expert", "hidden", None),
    )
    return jax.shard_map(
        body,
        mesh=mesh,
        in_specs=placed,
        out_specs=(P("expert", "hidden"), P("expert", None)),
        check_vma=False,
    )
```

```python
import jax
import jax.numpy as jnp
from jax import lax
from jax.experimental import pallas as pl
from jax.experimental.pallas import tpu as pltpu
from jax.sharding import PartitionSpec as P

MESH = pl.DeviceIdType.MESH
F32 = jnp.float32
BF16 = jnp.bfloat16

TD = 512
HALF = 256
NE = 16
EH = 8
SL = 48
SI = 24
NS = NE * SL
D = 3072
FB = 384
YB = 768
FH = 1024
RC = 256
PART = (0, 256, 384)


def nt(a, b):
    return lax.dot_general(a, b, (((1,), (1,)), ((), ())), preferred_element_type=F32)


def nn(a, b):
    return jnp.dot(a, b, preferred_element_type=F32)


def iota(shape, dim):
    return lax.broadcasted_iota(jnp.int32, shape, dim)


def one(cond):
    return jnp.where(cond, 1.0, 0.0).astype(F32)


def kernel(
    tok_h, og_h, gates, labels, tpk, ipk, mask, wg_h, wu_h, wd_h,
    ig, rg,
    wg, wu, wd, cols, tri, idn, mref, smat, s2mat, gmat, omat, pmat, ptmat,
    send_t, send_i, recv, x, acc, gd, ud, stage, crecv, fstage, ustage, dstage,
    arecv, brecv, urecv, drecv, rgm, vsend, vrecv, ssend, sland, srecv,
    ld_sem, w_sem, s1t, s1i, r1, sy, ry, sc, rc, ss, rs, scc, rcc, sab, rab, sud, rud,
    sv, rv,
):
    me = lax.axis_index("expert")
    h = lax.axis_index("hidden")
    y = lax.div(h, 2)
    c = lax.rem(h, 2)
    oc = 1 - c
    far = lax.rem(y + 2, 4)
    up = lax.rem(y + 1, 4)
    dn = lax.rem(y + 3, 4)
    kcol = lax.rem(me, EH)
    is_text = me < EH
    n_chunks = 2 - lax.div(me, EH)
    blocks = (y, far, up, dn)

    def remote(src, dst, s_sem, r_sem, **where):
        return pltpu.make_async_remote_copy(
            src_ref=src, dst_ref=dst, send_sem=s_sem, recv_sem=r_sem,
            device_id=where, device_id_type=MESH,
        )

    def colsl(core):
        return pl.ds(pl.multiple_of(core * FB, 128), FB)

    def rowsl(r):
        return pl.ds(pl.multiple_of(r * RC, RC), RC)

    leave = []
    text_gone = {}

    def both(rows_of):
        @pl.when(is_text)
        def _():
            rows_of(TD)

        @pl.when(jnp.logical_not(is_text))
        def _():
            rows_of(RC)

    loads = []
    for f, yy in enumerate((y, far)):
        fs = pl.ds(pl.multiple_of((yy * 2 + c) * FB, 128), FB)
        for a, src in enumerate((tok_h, og_h)):
            cp = pltpu.make_async_copy(
                src.at[:, fs], cols.at[f, pl.ds(a * TD, TD), :], ld_sem.at[f, a])
            cp.start()
            loads.append(cp)
    wloads = []
    for k, yy in enumerate(blocks):
        rows = pl.ds(pl.multiple_of(yy * YB, YB), YB)
        trio = [
            pltpu.make_async_copy(wg_h.at[rows, :], wg.at[rows, :], w_sem.at[k, 0]),
            pltpu.make_async_copy(wu_h.at[rows, :], wu.at[rows, :], w_sem.at[k, 1]),
            pltpu.make_async_copy(wd_h.at[:, rows], wd.at[:, rows], w_sem.at[k, 2]),
        ]
        for cp in trio:
            cp.start()
        wloads.append(trio)

    barrier = pltpu.get_barrier_semaphore()

    @pl.loop(1, NE)
    def _(k):
        pl.semaphore_signal(barrier, inc=1, device_id={"expert": lax.rem(me + k, NE)}, device_id_type=MESH)

    @pl.loop(1, 8)
    def _(k):
        pl.semaphore_signal(barrier, inc=1, device_id={"hidden": lax.rem(h + k, 8)}, device_id_type=MESH)

    r5 = iota((TD, TD), 0)
    c5 = iota((TD, TD), 1)
    tri[...] = one(r5 <= c5).astype(BF16)
    idn[...] = one(r5 == c5).astype(BF16)
    text = one(labels[...] == 0)
    lab16 = jnp.where(iota((NE, TD), 0) < EH, text, 1.0 - text)
    rank = nn(lab16.astype(BF16), tri[...])
    key = jnp.where(lab16 > 0.0, rank - 1.0, -1.0)

    def local_rank(p):
        return jnp.where(lax.shift_right_logical(p, 8) == me, (p & 255), -1).astype(F32)

    lov = jnp.concatenate([
        local_rank(tpk[...]),
        jnp.concatenate([local_rank(ipk[...]), jnp.full((EH, TD - HALF), -1.0, F32)], axis=1),
    ], axis=0)
    lov_t = nt(idn[...], lov.astype(BF16))
    rrow = iota((1, HALF), 1).astype(F32)
    def slots(e0, depth):
        for e in range(e0, e0 + EH):
            hit = one(lov_t[:depth, e:e + 1] == rrow)
            mref[e:e + 1, :] = jnp.sum(hit, axis=0, keepdims=True)
        member = mref[e0:e0 + EH, :]
        slot = member * nn(member.astype(BF16), tri[:HALF, :HALF])
        rcol = iota((HALF, TD), 0).astype(F32)
        return nn(slot.astype(BF16), one(rcol == key[e0:e0 + 1, :]).astype(BF16))

    st_text = slots(0, TD)
    s1 = iota((SL, TD), 0).astype(F32) + 1.0
    for e in range(EH):
        smat[e * SL:(e + 1) * SL, :] = one(st_text[e:e + 1, :] == s1).astype(BF16)

    pl.semaphore_wait(barrier, NE - 1 + 7)

    def text_copy(f, a, d):
        return remote(send_t.at[f, a, d], recv.at[f, a, me], s1t.at[f, a, d], r1.at[f, a, me], expert=d)

    def image_copy(f, d):
        return remote(send_i.at[f, d], recv.at[f, 0, me], s1i.at[f, d], r1.at[f, 0, me], expert=EH + d)

    def pick_text(f, a):
        loads[f * 2 + a].wait()
        t = nn(smat[...], cols[f, a * TD:(a + 1) * TD, :])
        send_t[f, a] = t.astype(BF16).reshape(EH, SL, FB)

        @pl.loop(0, EH)
        def _(k):
            d = lax.rem(me + k, EH)

            @pl.when(d != me)
            def _():
                text_copy(f, a, d).start()

            @pl.when(d == me)
            def _():
                recv[f, a, me] = send_t[f, a, d]

        def gone():
            @pl.loop(0, EH)
            def _(d):
                @pl.when(d != me)
                def _():
                    text_copy(f, a, d).wait_send()

        text_gone[f, a] = gone

    def left(f, a):
        text_gone.pop((f, a))()

    def pick_image(f):
        t = nn(s2mat[...], cols[f])
        send_i[f] = t.astype(BF16).reshape(EH, SL, FB)

        @pl.loop(0, EH)
        def _(k):
            d = lax.rem(me + k, EH)

            @pl.when(EH + d != me)
            def _():
                image_copy(f, d).start()

            @pl.when(EH + d == me)
            def _():
                recv[f, 0, me] = send_i[f, d]

        @leave.append
        def _():
            @pl.loop(0, EH)
            def _(d):
                @pl.when(EH + d != me)
                def _():
                    image_copy(f, d).wait_send()

    pick_text(0, 0)

    st_image = slots(EH, HALF)
    for e in range(EH):
        im = st_image[e:e + 1, :]
        s2mat[e * SL:(e + 1) * SL, :TD] = one(im == s1).astype(BF16)
        im2 = jnp.where(im > 0.0, im + SI, -1.0)
        s2mat[e * SL:(e + 1) * SL, TD:] = one(im2 == s1).astype(BF16)

    jq_row = jnp.floor((iota((1, NS), 1).astype(F32) + 0.5) * (1.0 / SL))
    jr_row = iota((1, NS), 1).astype(F32) - jq_row * SL
    jq_col = jnp.floor((iota((NS, 1), 0).astype(F32) + 0.5) * (1.0 / SL))
    jr_col = iota((NS, 1), 0).astype(F32) - jq_col * SL

    def source(p):
        return lax.shift_right_logical(p, 8).astype(F32)

    src_text = source(tpk[pl.ds(kcol, 1), :])
    src_image = jnp.concatenate(
        [source(ipk[pl.ds(kcol, 1), :]), jnp.full((1, TD - HALF), 99.0, F32)], axis=1)
    src = jnp.where(is_text, src_text, src_image)
    i16 = iota((NE, 1), 0).astype(F32)
    cnt16 = jnp.sum(one(src == i16), axis=1, keepdims=True)
    off16 = jnp.sum(one(src < i16), axis=1, keepdims=True)
    spread = iota((NE, NS), 0).astype(F32) == jq_row
    cnt_row = jnp.sum(jnp.where(spread, cnt16, 0.0), axis=0, keepdims=True)
    off_row = jnp.sum(jnp.where(spread, off16, 0.0), axis=0, keepdims=True)
    for a in range(2):
        shift = (lax.div(me, EH) * (SI * a)).astype(F32)
        place = jr_row - shift
        good = jnp.where((place >= 0.0) & (place < cnt_row), off_row + place, -1.0)
        pmat[a] = one(iota((TD, NS), 0).astype(F32) == good).astype(BF16)
    cnt_col = jnp.sum(one(src == jq_col), axis=1, keepdims=True)
    off_col = jnp.sum(one(src < jq_col), axis=1, keepdims=True)
    good_col = jnp.where(jr_col < cnt_col, off_col + jr_col, -1.0)
    ptmat[...] = one(iota((NS, TD), 1).astype(F32) == good_col).astype(BF16)

    def owner_tables():
        st = jnp.concatenate([st_text, st_image], axis=0)
        st_t = nt(idn[...], st.astype(BF16)).astype(BF16)
        st_wide = nn(st_t, one(spread).astype(BF16))
        filled = st_wide == jr_row + 1.0
        omat[...] = one(filled).astype(BF16)
        k_row = jnp.where(jq_row >= EH, jq_row - EH, jq_row)
        spread_k = one(iota((EH, NS), 0).astype(F32) == k_row).astype(BF16)
        gate_wide = nn(nt(idn[...], gates[...]).astype(BF16), spread_k)
        gmat[...] = jnp.where(filled, gate_wide, 0.0).astype(BF16)

    vrecv[EH:, 32:, :] = jnp.zeros((EH, SL - 32, FB), BF16)
    sland[EH:, 32:, :] = jnp.zeros((EH, SL - 32, 128), BF16)

    @pl.when(jnp.logical_not(is_text))
    def _():
        rgm[RC:, :] = jnp.zeros((TD - RC, FB), BF16)

    srecv[h] = jnp.zeros((1, TD), F32)

    def y_copy(a, r, way):
        ref = x.at[a, y, rowsl(r), colsl(c)]
        return remote(ref, ref, sy.at[a, r, way], ry.at[a, r, way], hidden=(up, dn)[way] * 2 + c)

    def y_wait(a, r, way):
        ref = x.at[a, (dn, up)[way], rowsl(r), colsl(c)]
        remote(ref, ref, sy.at[a, r, way], ry.at[a, r, way], hidden=(dn, up)[way] * 2 + c).wait_recv()

    def core_copy(a, k, r):
        ref = x.at[a, blocks[k], rowsl(r), colsl(c)]
        return remote(ref, ref, sc.at[a, k, r], rc.at[a, k, r], hidden=y * 2 + oc)

    def core_wait(a, k, r):
        ref = x.at[a, blocks[k], rowsl(r), colsl(oc)]
        remote(ref, ref, sc.at[a, k, r], rc.at[a, k, r], hidden=y * 2 + oc).wait_recv()

    def chunks_left(*copies, only=None):
        def wait():
            @pl.loop(0, n_chunks)
            def _(r):
                for copy in copies:
                    copy(r).wait_send()

        leave.append(wait if only is None else lambda: pl.when(only)(wait))

    def compact(f, a, text_expert):
        aa = a if text_expert else 0

        @pl.when(is_text if text_expert else jnp.logical_not(is_text))
        def _():
            if text_expert or a == 0:
                @pl.loop(0, NE)
                def _(s):
                    @pl.when(s != me)
                    def _():
                        remote(send_t.at[f, a, 0], recv.at[f, aa, s], s1t.at[f, a, 0], r1.at[f, aa, s],
                               expert=s).wait_recv()

            @pl.loop(0, 2 if text_expert else 1)
            def _(r):
                got = nn(pmat[a, rowsl(r), :], recv[f, aa].reshape(NS, FB))
                x[a, blocks[f], rowsl(r), colsl(c)] = got.astype(BF16)
                if f == 0:
                    y_copy(a, r, 0).start()
                    y_copy(a, r, 1).start()
                core_copy(a, f, r).start()

        copies = [lambda r: core_copy(a, f, r)]
        if f == 0:
            copies += [lambda r: y_copy(a, r, 0), lambda r: y_copy(a, r, 1)]
        chunks_left(*copies, only=is_text if text_expert else jnp.logical_not(is_text))

    def forward(a, k):
        @pl.loop(0, n_chunks)
        def _(r):
            y_wait(a, r, 1 if k == 2 else 0)
            core_copy(a, k, r).start()

        chunks_left(lambda r: core_copy(a, k, r))

    def project(a, k):
        yy = blocks[k]
        rows = pl.ds(pl.multiple_of(yy * YB, YB), YB)
        if a == 0:
            wloads[k][0].wait()
            wloads[k][1].wait()
        else:
            wloads[k][2].wait()

        @pl.loop(0, n_chunks)
        def _(r):
            core_wait(a, k, r)

        def rows_of(m):
            left = x[a, yy, :m, :]
            for n in range(FH // 256):
                ns = pl.ds(n * 256, 256)
                if a == 0:
                    outs = ((0, nn(left, wg[rows, ns])), (1, nn(left, wu[rows, ns])))
                else:
                    outs = ((2, nt(left, wd[ns, rows])),)
                for i, v in outs:
                    if k == 0:
                        acc[i, :m, ns] = v
                    else:
                        acc[i, :m, ns] += v

        both(rows_of)

    pick_text(0, 1)
    pick_image(0)
    pick_text(1, 0)
    compact(0, 0, True)
    left(0, 0)
    left(0, 1)
    pick_text(1, 1)
    pick_image(1)
    compact(0, 1, True)
    compact(0, 0, False)
    compact(0, 1, False)
    owner_tables()
    project(0, 0)
    forward(0, 2)
    forward(0, 3)
    compact(1, 0, True)
    project(1, 0)
    project(0, 2)
    project(0, 3)
    compact(1, 0, False)
    compact(1, 1, False)
    compact(1, 1, True)
    forward(1, 2)
    forward(1, 3)
    project(0, 1)
    project(1, 1)
    project(1, 2)
    project(1, 3)

    keep = jnp.concatenate(
        [jnp.broadcast_to(mask[:, j:j + 1].astype(F32), (1, 128)) for j in range(8)], axis=1)
    eye = iota((128, 128), 0) == iota((128, 128), 1)

    @pl.loop(0, n_chunks * 2)
    def _(i):
        rows = pl.ds(pl.multiple_of(i * 128, 128), 128)
        gate_in = acc[0, rows, :]
        up_in = acc[1, rows, :]
        back = acc[2, rows, :]
        sig = jax.nn.sigmoid(gate_in)
        swish = gate_in * sig
        slope = sig * (1.0 + gate_in * (1.0 - sig))
        act = (swish * up_in * keep).astype(BF16).astype(F32)
        score = jnp.sum(act * back, axis=1, keepdims=True)
        hidden = back * keep
        gd[rows, :] = (hidden * up_in * slope).astype(BF16)
        ud[rows, :] = (hidden * swish).astype(BF16)
        srecv[h, :, pl.ds(pl.multiple_of(i * 128, 128), 128)] = jnp.sum(
            jnp.where(eye, score, 0.0), axis=0, keepdims=True)

    def score_copy(k):
        to = lax.rem(h + k, 8)
        return remote(srecv.at[h], srecv.at[h], ss.at[to], rs.at[h], hidden=to)

    @pl.loop(1, 8)
    def _(k):
        score_copy(k).start()

    @leave.append
    def _():
        @pl.loop(1, 8)
        def _(k):
            score_copy(k).wait_send()

    order = (1, 2, 3, 0)

    def part(s):
        return slice(PART[s], PART[s + 1])

    def kept(s, j):
        return j // 2, slice(j % 2 * FB + PART[s], j % 2 * FB + PART[s + 1])

    def pair_copy(s, j, n):
        ref = stage.at[j, pl.ds(0, n), part(s)], crecv.at[j, pl.ds(0, n), part(s)]
        return remote(*ref, scc.at[s, j], rcc.at[s, j], hidden=y * 2 + oc)

    def half(way, n):
        return pl.ds(way * (n // 2), n // 2)

    def half_copy(s, way, n):
        land = (arecv, brecv)[way]
        return remote(fstage.at[half(way, n), part(s)], land.at[pl.ds(0, n // 2), part(s)],
                      sab.at[s, way], rab.at[s, way], hidden=(up, dn)[way] * 2 + c)

    def full_copy(s, way, m, n):
        return remote((ustage, dstage)[way].at[half(m, n), part(s)], (urecv, drecv)[way].at[half(m, n), part(s)],
                      sud.at[s, way, m], rud.at[s, way, m], hidden=(up, dn)[way] * 2 + c)

    def later(copy):
        leave.append(lambda: both(lambda n: copy(n).wait_send()))

    def terms(s, j):
        wide = PART[s + 1] - PART[s]
        base = blocks[order[j]] * YB + PART[s]
        mine = pl.ds(pl.multiple_of(base + c * FB, 128), wide)
        other = pl.ds(pl.multiple_of(base + oc * FB, 128), wide)
        at, lanes = kept(s, j)

        def rows_of(n):
            wgs = jnp.concatenate([wg[mine, :], wg[other, :]], axis=0)
            wus = jnp.concatenate([wu[mine, :], wu[other, :]], axis=0)
            v = nt(gd[:n, :], wgs) + nt(ud[:n, :], wus)
            stage[j, :n, part(s)] = v[:, wide:].astype(BF16)
            pair_copy(s, j, n).start()
            acc[at, :n, lanes] = v[:, :wide]

        both(rows_of)
        later(lambda n: pair_copy(s, j, n))

    def pair_sum(s, j, m, n):
        at, lanes = kept(s, j)
        return acc[at, half(m, n), lanes] + crecv[j, half(m, n), part(s)].astype(F32)

    def finish_far(s):
        def rows_of(n):
            pair_copy(s, 0, n).wait_recv()
            for way in range(2):
                fstage[half(way, n), part(s)] = pair_sum(s, 0, way, n).astype(BF16)
                half_copy(s, way, n).start()

        both(rows_of)
        later(lambda n: half_copy(s, 0, n))
        later(lambda n: half_copy(s, 1, n))

    def finish_free(s, way):
        def rows_of(n):
            pair_copy(s, 1 + way, n).wait_recv()
            (ustage, dstage)[way][half(1 - way, n), part(s)] = pair_sum(s, 1 + way, 1 - way, n).astype(BF16)
            full_copy(s, way, 1 - way, n).start()

        both(rows_of)
        later(lambda n: full_copy(s, way, 1 - way, n))

    def finish_rest(s, way):
        def rows_of(n):
            half_copy(s, way, n).wait_recv()
            v = pair_sum(s, 1 + way, way, n) + (arecv, brecv)[way][:n // 2, part(s)].astype(F32)
            (ustage, dstage)[way][half(way, n), part(s)] = v.astype(BF16)
            full_copy(s, way, way, n).start()

        both(rows_of)
        later(lambda n: full_copy(s, way, way, n))

    def finish_own(s):
        def rows_of(n):
            pair_copy(s, 3, n).wait_recv()
            for m in (1, 0):
                full_copy(s, 0, m, n).wait_recv()
                full_copy(s, 1, m, n).wait_recv()
                v = pair_sum(s, 3, m, n)
                v = v + urecv[half(m, n), part(s)].astype(F32) + drecv[half(m, n), part(s)].astype(F32)
                rgm[half(m, n), part(s)] = v.astype(BF16)

        both(rows_of)

    def row_copy(p, d, n):
        if p == len(PART) - 1:
            src, dst = ssend.at[d, pl.ds(0, n), :], sland.at[me, pl.ds(0, n), :]
        else:
            src, dst = vsend.at[d, pl.ds(0, n), part(p)], vrecv.at[me, pl.ds(0, n), part(p)]
        return remote(src, dst, sv.at[p, d], rv.at[p, me], expert=d)

    def row_wait(p, n, first, last):
        @pl.loop(first, last)
        def _(s):
            @pl.when(s != me)
            def _():
                if p == len(PART) - 1:
                    src, dst = ssend.at[s, pl.ds(0, n), :], sland.at[s, pl.ds(0, n), :]
                else:
                    src, dst = vsend.at[s, pl.ds(0, n), part(p)], vrecv.at[s, pl.ds(0, n), part(p)]
                remote(src, dst, sv.at[p, s], rv.at[p, s], expert=s).wait_recv()

    def row_send(p):
        def all_rows(act):
            @pl.when(is_text)
            def _():
                @pl.loop(1, NE)
                def _(k):
                    act(row_copy(p, lax.rem(me + k, NE), SL))

            @pl.when(jnp.logical_not(is_text))
            def _():
                @pl.loop(1, NE)
                def _(k):
                    act(row_copy(p, lax.rem(me + k, NE), 32))

        all_rows(lambda copy: copy.start())
        src, dst, lanes = (ssend, sland, slice(None)) if p == len(PART) - 1 else (vsend, vrecv, part(p))
        dst[me, :32, lanes] = src[me, :32, lanes]

        @pl.when(is_text)
        def _():
            dst[me, 32:, lanes] = src[me, 32:, lanes]

        leave.append(lambda: all_rows(lambda copy: copy.wait_send()))

    def send_scores():
        @pl.loop(1, 8)
        def _(k):
            frm = lax.rem(h + k, 8)
            remote(srecv.at[h], srecv.at[frm], ss.at[frm], rs.at[frm], hidden=frm).wait_recv()

        total = srecv[0]
        for k in range(1, 8):
            total = total + srecv[k]
        total = total.astype(BF16).astype(F32)
        for q in range(4):
            rows = pl.ds(q * (NS // 4), NS // 4)
            scol = jnp.sum(ptmat[rows, :].astype(F32) * total, axis=1, keepdims=True)
            put = jnp.where(iota((NS // 4, 128), 1) == kcol, scol, 0.0).astype(BF16)
            ssend[pl.ds(q * 4, 4)] = put.reshape(4, SL, 128)
        row_send(len(PART) - 1)

    def send_rows(s):
        finish_own(s)
        wide = PART[s + 1] - PART[s]
        vsend[:, :, part(s)] = nn(ptmat[...], rgm[:, part(s)]).astype(BF16).reshape(NE, SL, wide)
        row_send(s)

    def scores_here():
        row_wait(len(PART) - 1, SL, 0, EH)
        row_wait(len(PART) - 1, 32, EH, NE)
        rg[...] = jnp.transpose(nn(omat[...], sland[...].reshape(NS, 128)))[:EH].astype(BF16)

    def rows_here(s):
        row_wait(s, SL, 0, EH)
        row_wait(s, 32, EH, NE)
        wide = PART[s + 1] - PART[s]
        ig[:, part(s)] = nn(gmat[...], vrecv[:, :, part(s)].reshape(NS, wide)).astype(BF16)

    def flush():
        for wait in leave + list(text_gone.values()):
            wait()
        leave.clear()
        text_gone.clear()

    terms(0, 0)
    terms(0, 1)
    finish_far(0)
    terms(0, 2)
    finish_free(0, 0)
    terms(1, 0)
    finish_free(0, 1)
    finish_rest(0, 0)
    finish_rest(0, 1)
    finish_far(1)
    terms(0, 3)
    terms(1, 1)
    send_scores()
    terms(1, 2)
    finish_free(1, 0)
    finish_free(1, 1)
    finish_rest(1, 0)
    finish_rest(1, 1)
    send_rows(0)
    terms(1, 3)
    flush()
    send_rows(1)
    scores_here()
    rows_here(0)
    rows_here(1)

    flush()


def body(tokens, out_grad, gates, labels, text_picks, image_picks, block_mask, w_gate, w_up, w_down):
    any_spec = pl.BlockSpec(memory_space=pl.ANY)
    vmem = pl.BlockSpec(memory_space=pltpu.VMEM)
    dma = pltpu.SemaphoreType.DMA
    input_grad, router_grad = pl.pallas_call(
        kernel,
        out_shape=(
            jax.ShapeDtypeStruct((TD, FB), BF16),
            jax.ShapeDtypeStruct((EH, TD), BF16),
        ),
        in_specs=[any_spec, any_spec, vmem, vmem, vmem, vmem, vmem, any_spec, any_spec, any_spec],
        out_specs=(vmem, vmem),
        scratch_shapes=[
            pltpu.VMEM((D, FH), BF16),
            pltpu.VMEM((D, FH), BF16),
            pltpu.VMEM((FH, D), BF16),
            pltpu.VMEM((2, 2 * TD, FB), BF16),
            pltpu.VMEM((TD, TD), BF16),
            pltpu.VMEM((TD, TD), BF16),
            pltpu.VMEM((NE, HALF), F32),
            pltpu.VMEM((EH * SL, TD), BF16),
            pltpu.VMEM((EH * SL, 2 * TD), BF16),
            pltpu.VMEM((TD, NS), BF16),
            pltpu.VMEM((TD, NS), BF16),
            pltpu.VMEM((2, TD, NS), BF16),
            pltpu.VMEM((NS, TD), BF16),
            pltpu.VMEM((2, 2, EH, SL, FB), BF16),
            pltpu.VMEM((2, EH, SL, FB), BF16),
            pltpu.VMEM((2, 2, NE, SL, FB), BF16),
            pltpu.VMEM((2, 4, TD, YB), BF16),
            pltpu.VMEM((3, TD, FH), F32),
            pltpu.VMEM((TD, FH), BF16),
            pltpu.VMEM((TD, FH), BF16),
            pltpu.VMEM((4, TD, FB), BF16),
            pltpu.VMEM((4, TD, FB), BF16),
            pltpu.VMEM((TD, FB), BF16),
            pltpu.VMEM((TD, FB), BF16),
            pltpu.VMEM((TD, FB), BF16),
            pltpu.VMEM((TD // 2, FB), BF16),
            pltpu.VMEM((TD // 2, FB), BF16),
            pltpu.VMEM((TD, FB), BF16),
            pltpu.VMEM((TD, FB), BF16),
            pltpu.VMEM((TD, FB), BF16),
            pltpu.VMEM((NE, SL, FB), BF16),
            pltpu.VMEM((NE, SL, FB), BF16),
            pltpu.VMEM((NE, SL, 128), BF16),
            pltpu.VMEM((NE, SL, 128), BF16),
            pltpu.VMEM((8, 1, TD), F32),
            dma((2, 2)),
            dma((4, 3)),
            dma((2, 2, EH)),
            dma((2, EH)),
            dma((2, 2, NE)),
            dma((2, 2, 2)),
            dma((2, 2, 2)),
            dma((2, 4, 2)),
            dma((2, 4, 2)),
            dma((8,)),
            dma((8,)),
            dma((2, 4)),
            dma((2, 4)),
            dma((2, 2)),
            dma((2, 2)),
            dma((2, 2, 2)),
            dma((2, 2, 2)),
            dma((3, NE)),
            dma((3, NE)),
        ],
        compiler_params=pltpu.CompilerParams(
            collective_id=0, has_side_effects=True, vmem_limit_bytes=62 * 1024 * 1024),
        cost_estimate=pl.CostEstimate(flops=16_000_000_000, bytes_accessed=22_000_000, transcendentals=1_000_000),
    )(
        tokens, out_grad, gates.T, labels.reshape(1, TD), text_picks, image_picks, block_mask,
        w_gate[0], w_up[0], w_down[0],
    )
    return input_grad, router_grad.T


def solution(mesh):
    placed = (
        P("expert", None),
        P("expert", None),
        P("expert", None),
        P("expert"),
        P(),
        P(),
        P("expert", "hidden"),
        P("expert", None, "hidden"),
        P("expert", None, "hidden"),
        P("expert", "hidden", None),
    )
    return jax.shard_map(
        body,
        mesh=mesh,
        in_specs=placed,
        out_specs=(P("expert", "hidden"), P("expert", None)),
        check_vma=False,
    )
```
